32 devices in a mesh: dp: 8 (over z, x), tensor: 4 (over y, core).
Axes of the slice: x: 2, y: 2, z: 4, core: 2. Of those that a mesh axis runs over, the one named last changes fastest.
Arguments:
- projections: bfloat16 [3072, 3, 3072], P('dp', None, 'tensor'), may hold values from -5.5 to 5.5
- routes: int32 [3072, 1], replicated, may hold values from 0 to 7; in each aligned block of 384 rows (0 to 383, 384 to 767, ...) at most 64 rows name the same one
- segments: int32 [8, 512], P('dp'), may hold values from 0 to 15, never falling along the last dimension, each value on 1 to 128 neighbouring positions
- out_weight: bfloat16 [3072, 6144], P('tensor'), may hold values from -0.109375 to 0.109375
Outputs:
- attention_out: bfloat16 [3072, 6144], P('dp', 'tensor')
The draws below stay inside these ranges and needn't reach their ends.
Inputs may be any that keep to these rules, and one draw needn't show every extreme that they name: `routes`: at most 64 of the 384 rows of one device name the same sequence, and in every draw the rows of some device name some sequence exactly 64 times. `segments`: in each row the image numbers never fall, each image covers 1 to 128 positions, and one image covers exactly 128.
All inputs are finite; a program needn't handle non-finite values.
Results may differ from the reference program's by a relative error of at most 0.009.
Values may be sent and summed in bfloat16 or wider, within the bound.
A program may use at most 64 MiB of HBM per device.

```python
import math
import jax
import jax.numpy as jnp
import numpy as np
from jax import lax

D = 6144
HD = 128
HEADS = 24
OWN = 384
MAXP = 128
TOKENS = 3072
SLOT = 64
SEQ_POS = 512
SEGS = 16
N_DP = 8
N_TENSOR = 4


def draw_projections(key, part):
    full_shape = (TOKENS, 3, HEADS * HD)
    sub_keys = jax.random.split(key, 1)
    result = jnp.clip(jax.random.normal(sub_keys[0], full_shape, jnp.float32), -5.0, 5.0)
    return result.astype(jnp.bfloat16)


def level_of(rng, shape, cuts, smallest, high):
    factor_of, own = 1.0, jax.random.fold_in(rng, 6)
    for axis_at, parts in cuts:
        draws = jnp.exp(jax.random.uniform(jax.random.fold_in(own, axis_at), (parts,), jnp.float32, smallest / len(cuts), high / len(cuts)))
        factor_of = factor_of * jnp.repeat(draws, shape[axis_at] // parts).reshape([-1 if axis == axis_at else 1 for axis in range(len(shape))])
    return factor_of


def length_profile(amount, total, reach, lean):
    portions = [(1 << 20) // math.isqrt(rank ** lean) + 1 for rank in range(2, amount + 1)]
    surplus, counts = total - reach - (amount - 1), [1] * (amount - 1)
    while surplus > 0:
        candidates = [i for i in range(amount - 1) if counts[i] < reach]
        mass, left = sum([portions[i] for i in candidates]), surplus
        for i in candidates:
            extra = min(reach - counts[i], max(1, left * portions[i] // mass), surplus)
            counts[i] = counts[i] + extra
            surplus = surplus - extra
    return np.array([reach] + counts)


def uneven(stream_key, count, total, bound, skew):
    if count == 2:
        one = jax.random.randint(stream_key, (), max(1, total - bound), min(bound, total - 1) + 1)
        return jnp.stack([one, total - one])
    lengths = jnp.asarray(length_profile(count, total, bound, skew), jnp.int32)
    pairs = (count - 1) // 2
    giver, sink = lengths[1:1 + 2 * pairs:2], lengths[2:2 + 2 * pairs:2]
    slack = jnp.minimum(giver - 1, bound - sink)
    shifted = jax.random.randint(jax.random.fold_in(stream_key, 1), (pairs,), 0, 1 << 20) % (slack + 1)
    lengths = lengths.at[1:1 + 2 * pairs:2].set(giver - shifted).at[2:2 + 2 * pairs:2].set(sink + shifted)
    return lengths[jax.random.permutation(jax.random.fold_in(stream_key, 2), count)]


def assign_block(stream_key, own, number, rows, amount, top, reach, lean):
    ranking = jax.random.permutation(stream_key, amount)
    packed, ordinary = portions_of(amount, rows * top, reach, lean, True), portions_of(amount, rows * top, reach, lean, False)
    places = jnp.arange(amount)

    def named(sizes, offset_by):
        used = int((sizes > 0).sum())
        fixed = max(1, used // 4)
        shifted = fixed + (places - fixed + offset_by * (used - fixed)) % max(1, amount - fixed)
        return jnp.zeros((amount,), jnp.int32).at[ranking[jnp.where(places < fixed, places, shifted)]].set(jnp.asarray(sizes, jnp.int32))

    sizes = jnp.where(number % 4 == 0, named(packed, number // 4), named(ordinary, number - number // 4 - 1))
    mixed = jax.random.permutation(jax.random.fold_in(own, 3), amount)
    giver, sink = mixed[0:amount // 2 * 2:2], mixed[1:amount // 2 * 2:2]
    margin = jnp.minimum(sizes[giver] - 1, reach - sizes[sink]) // 2
    margin = jnp.where((giver == ranking[0]) | (sink == ranking[0]) | (sizes[sink] == 0), 0, jnp.maximum(margin, 0))
    shifted = jax.random.randint(jax.random.fold_in(own, 4), (amount // 2,), 0, 1 << 20) % (margin + 1)
    sizes = sizes.at[giver].add(-shifted).at[sink].add(shifted)
    members = jnp.searchsorted(jnp.cumsum(sizes), jnp.arange(rows * top), side="right").astype(jnp.int32)
    listing = members.reshape(top, rows).T
    listing = listing[jax.random.permutation(jax.random.fold_in(own, 1), rows)]
    offset_by = jax.random.randint(jax.random.fold_in(own, 2), (rows, 1), 0, top)
    return jnp.take_along_axis(listing, (jnp.arange(top)[None, :] + offset_by) % top, axis=1)


def portions_of(amount, total, limit, skew, full):
    weights = [(1 << 20) // math.isqrt(rank ** skew) + 1 for rank in range(1, amount + 1)]
    largest = limit if full else min(limit, max(-(-total // amount), total * weights[0] // sum(weights)))
    least = 1 if total - largest >= amount - 1 else 0
    counts, surplus = [largest] + [least] * (amount - 1), total - largest - least * (amount - 1)
    while surplus > 0:
        movable = [i for i in range(1, amount) if counts[i] < largest] or [i for i in range(1, amount) if counts[i] < limit]
        mass, remaining = sum([weights[i] for i in movable]), surplus
        for i in movable:
            addition = min(limit - counts[i], max(1, remaining * weights[i] // mass), surplus)
            counts[i] = counts[i] + addition
            surplus = surplus - addition
    return np.array(counts)


def centred(rng, dims, scale, limit, shards=(), held_as=jnp.bfloat16):
    values = jax.random.normal(rng, dims, jnp.float32) * scale
    if len(shards) > 0:
        values = level_of(rng, dims, shards, -0.22, 0.18) * values
    return jnp.clip(values, min=-limit, max=limit).astype(held_as)


def setup_inputs(seed: int = 0) -> dict:
    streams_of = jax.random.split(jax.random.key(seed), 5)
    projections = draw_projections(jax.random.fold_in(streams_of[4], 71), 0)
    routes_keys = jax.random.split(jax.random.fold_in(streams_of[1], 1), TOKENS // OWN)
    routes_turns = jax.random.permutation(jax.random.fold_in(streams_of[1], 3), TOKENS // OWN)
    routes = jax.vmap(lambda own, number: assign_block(jax.random.fold_in(streams_of[1], 2), own, number, OWN, N_DP, 1, SLOT, 2))(routes_keys, routes_turns).reshape((TOKENS, 1))
    segments = jax.vmap(lambda own: jnp.searchsorted(jnp.cumsum(uneven(own, SEGS, SEQ_POS, MAXP, 2)), jnp.arange(SEQ_POS), side="right"))(jax.random.split(streams_of[2], N_DP)).reshape((N_DP, SEQ_POS)).astype(jnp.int32)
    out_weight = centred(streams_of[3], (HEADS * HD, D), (HEADS * HD) ** -0.5, 0.109375, ((0, 4),))
    return {"projections": projections, "routes": routes, "segments": segments, "out_weight": out_weight}


def attend_sequence(block_pair):
    packed_rows, group_ids = block_pair
    queries = packed_rows[:, 0].astype(jnp.float32)
    keys_in = packed_rows[:, 1].astype(jnp.float32)
    values_in = packed_rows[:, 2].astype(jnp.float32)
    allowed = group_ids[:, None] == group_ids[None, :]
    scores = jnp.einsum('qhd,khd->hqk', queries, keys_in) * (1.0 / math.sqrt(HD))
    scores = jnp.where(allowed[None], scores, -jnp.inf)
    highest = lax.optimization_barrier(jnp.max(scores, axis=2, keepdims=True))
    raised = jnp.exp(scores - highest)
    weights = (raised / lax.optimization_barrier(jnp.sum(raised, axis=2, keepdims=True))).astype(jnp.bfloat16)
    weights = lax.optimization_barrier(weights)
    attended = jnp.einsum('hqk,khd->qhd', weights.astype(jnp.float32), values_in)
    return attended.astype(jnp.bfloat16)

def reference(projections, routes, segments, out_weight):
    targets = routes[:, 0]
    one_hot = (targets[:, None] == jnp.arange(N_DP, dtype=jnp.int32)[None, :]).astype(jnp.int32)
    position = lax.optimization_barrier(jnp.sum((jnp.cumsum(one_hot, axis=0) - one_hot) * one_hot, axis=1)).astype(jnp.int32)
    flat_slot = (targets * SEQ_POS + position).astype(jnp.int32)
    source_row = jnp.zeros((N_DP * SEQ_POS,), jnp.int32).at[flat_slot].set(jnp.arange(TOKENS, dtype=jnp.int32))
    filled = jnp.zeros((N_DP * SEQ_POS,), jnp.int32).at[flat_slot].set(1).reshape(N_DP, SEQ_POS)
    gathered = projections[source_row].reshape(N_DP, SEQ_POS, 3, HEADS, HD)
    unique_ids = -1 - jnp.arange(SEQ_POS, dtype=jnp.int32)
    group_ids = jnp.where(filled > 0, segments, unique_ids[None, :])
    per_sequence = lax.map(attend_sequence, (gathered, group_ids))
    attended = per_sequence.reshape(N_DP * SEQ_POS, HEADS * HD)[flat_slot]
    columns = HEADS * HD // N_TENSOR
    total = jnp.zeros((TOKENS, D), jnp.float32)
    for group in range(N_TENSOR):
        piece = jnp.dot(attended[:, group * columns:(group + 1) * columns], out_weight[group * columns:(group + 1) * columns], preferred_element_type=jnp.float32).astype(jnp.bfloat16)
        piece = lax.optimization_barrier(piece)
        total = total + piece.astype(jnp.float32)
    return total.astype(jnp.bfloat16)
```

```python
import functools
import math

import jax
import jax.numpy as jnp
from jax import lax
from jax.experimental import pallas as pl
from jax.experimental.pallas import tpu as pltpu
from jax.sharding import PartitionSpec as P

HD = 128


def routing(routes, segments, own_rows, senders, capacity):
    positions = senders * capacity
    myself = lax.axis_index("dp")
    targets = routes[:, 0]
    mine = lax.dynamic_slice_in_dim(targets, myself * own_rows, own_rows)
    row = jnp.arange(own_rows, dtype=jnp.int32)
    same_before = (mine[:, None] == mine[None, :]) & (row[None, :] < row[:, None])
    slot_of_row = mine * capacity + jnp.sum(same_before.astype(jnp.int32), axis=1)
    arrivals = jnp.sum((targets.reshape(senders, own_rows) == myself).astype(jnp.int32), axis=1)
    device = jnp.arange(senders, dtype=jnp.int32)
    earlier = jnp.sum(jnp.where(device[None, :] < device[:, None], arrivals[None, :], 0), axis=1)
    within = jnp.arange(capacity, dtype=jnp.int32)
    placed = (earlier[:, None] + within[None, :]).reshape(positions)
    filled = (within[None, :] < arrivals[:, None]).reshape(positions)
    flat = jnp.arange(positions, dtype=jnp.int32)
    looked_up = jnp.sum(jnp.where(placed[:, None] == flat[None, :], segments[0][None, :], 0), axis=1)
    return slot_of_row, jnp.where(filled, looked_up, -1 - flat)


def attend_heads(arrived, group_ids):
    slot_total, _, heads_now, head_size = arrived.shape
    block_rows = min(slot_total, 512)
    block_count = slot_total // block_rows
    queries = arrived[:, 0].reshape(block_count, block_rows, heads_now, head_size)
    query_ids = group_ids.reshape(block_count, block_rows)
    keys_in, values_in = arrived[:, 1], arrived[:, 2]
    scale = 1.0 / math.sqrt(head_size)

    def one_block(block_pair):
        query_block, ids = block_pair
        scores = jnp.einsum("qhd,khd->hqk", query_block, keys_in, preferred_element_type=jnp.float32) * scale
        scores = jnp.where((ids[:, None] == group_ids[None, :])[None], scores, -jnp.inf)
        raised = jnp.exp(scores - jnp.max(scores, axis=2, keepdims=True))
        weights = (raised / jnp.sum(raised, axis=2, keepdims=True)).astype(jnp.bfloat16)
        return jnp.einsum("hqk,khd->qhd", weights, values_in, preferred_element_type=jnp.float32).astype(jnp.bfloat16)

    return lax.map(one_block, (queries, query_ids)).reshape(slot_total, heads_now * head_size)


def local(projections, routes, segments, out_weight):
    senders = lax.axis_size("dp")
    own_rows, _, columns = projections.shape
    heads_here = columns // HD
    positions = segments.shape[1]
    capacity = positions // senders
    slot_of_row, group_ids = routing(routes, segments, own_rows, senders, capacity)
    source_row = jnp.zeros((positions,), jnp.int32).at[slot_of_row].set(jnp.arange(own_rows, dtype=jnp.int32))
    outgoing = projections[source_row].reshape(senders, capacity, 3, heads_here, HD)
    arrived = lax.all_to_all(outgoing, "dp", split_axis=0, concat_axis=0, tiled=True)
    attended = attend_heads(arrived.reshape(positions, 3, heads_here, HD), group_ids)
    returned = lax.all_to_all(
        attended.reshape(senders, capacity, columns), "dp", split_axis=0, concat_axis=0, tiled=True
    )
    own = returned.reshape(positions, columns)[slot_of_row]
    partial_value = jnp.dot(own, out_weight, preferred_element_type=jnp.float32)
    return lax.psum_scatter(partial_value.astype(jnp.bfloat16), "tensor", scatter_dimension=1, tiled=True)


def solution(mesh):
    in_specs = (P("dp", None, "tensor"), P(), P("dp", None), P("tensor", None))
    out_specs = P("dp", "tensor")
    return jax.shard_map(local, mesh=mesh, in_specs=in_specs, out_specs=out_specs, check_vma=False)
```

```python
import functools
import math

import jax
import jax.numpy as jnp
from jax import lax
from jax.experimental import pallas as pl
from jax.experimental.pallas import tpu as pltpu
from jax.sharding import PartitionSpec as P

HD = 128


def routing(routes, segments, own_rows, senders, capacity):
    positions = senders * capacity
    myself = lax.axis_index("dp")
    targets = routes[:, 0]
    mine = lax.dynamic_slice_in_dim(targets, myself * own_rows, own_rows)
    row = jnp.arange(own_rows, dtype=jnp.int32)
    same_before = (mine[:, None] == mine[None, :]) & (row[None, :] < row[:, None])
    slot_of_row = mine * capacity + jnp.sum(same_before.astype(jnp.int32), axis=1)
    arrivals = jnp.sum((targets.reshape(senders, own_rows) == myself).astype(jnp.int32), axis=1)
    device = jnp.arange(senders, dtype=jnp.int32)
    earlier = jnp.sum(jnp.where(device[None, :] < device[:, None], arrivals[None, :], 0), axis=1)
    within = jnp.arange(capacity, dtype=jnp.int32)
    placed = (earlier[:, None] + within[None, :]).reshape(positions)
    filled = (within[None, :] < arrivals[:, None]).reshape(positions)
    flat = jnp.arange(positions, dtype=jnp.int32)
    looked_up = jnp.sum(jnp.where(placed[:, None] == flat[None, :], segments[0][None, :], 0), axis=1)
    return slot_of_row, jnp.where(filled, looked_up, -1 - flat)


def attend_heads(arrived, group_ids):
    slot_total, _, heads_now, head_size = arrived.shape
    block_rows = min(slot_total, 512)
    block_count = slot_total // block_rows
    queries = arrived[:, 0].reshape(block_count, block_rows, heads_now, head_size)
    query_ids = group_ids.reshape(block_count, block_rows)
    keys_in, values_in = arrived[:, 1], arrived[:, 2]
    scale = 1.0 / math.sqrt(head_size)

    def one_block(block_pair):
        query_block, ids = block_pair
        scores = jnp.einsum("qhd,khd->hqk", query_block, keys_in, preferred_element_type=jnp.float32) * scale
        scores = jnp.where((ids[:, None] == group_ids[None, :])[None], scores, -jnp.inf)
        raised = jnp.exp(scores - jnp.max(scores, axis=2, keepdims=True))
        weights = (raised / jnp.sum(raised, axis=2, keepdims=True)).astype(jnp.bfloat16)
        return jnp.einsum("hqk,khd->qhd", weights, values_in, preferred_element_type=jnp.float32).astype(jnp.bfloat16)

    return lax.map(one_block, (queries, query_ids)).reshape(slot_total, heads_now * head_size)


def local(projections, routes, segments, out_weight):
    senders = lax.axis_size("dp")
    own_rows, _, columns = projections.shape
    heads_here = columns // HD
    positions = segments.shape[1]
    capacity = positions // senders
    slot_of_row, group_ids = routing(routes, segments, own_rows, senders, capacity)
    source_row = jnp.zeros((positions,), jnp.int32).at[slot_of_row].set(jnp.arange(own_rows, dtype=jnp.int32))
    outgoing = projections[source_row].reshape(senders, capacity, 3, heads_here, HD)
    arrived = lax.all_to_all(outgoing, "dp", split_axis=0, concat_axis=0, tiled=True)
    attended = attend_heads(arrived.reshape(positions, 3, heads_here, HD), group_ids)
    returned = lax.all_to_all(
        attended.reshape(senders, capacity, columns), "dp", split_axis=0, concat_axis=0, tiled=True
    )
    own = returned.reshape(positions, columns)[slot_of_row]
    partial_value = jnp.dot(own, out_weight, preferred_element_type=jnp.float32)
    return lax.psum_scatter(partial_value.astype(jnp.bfloat16), "tensor", scatter_dimension=1, tiled=True)


def xor(index, mask, size):
    result, bit = 0, 1
    while bit < size:
        digit = (index // bit) % 2
        result = result + ((1 - digit) if (mask // bit) % 2 else digit) * bit
        bit *= 2
    return result


def fused_kernel(
    senders, heads_step,
    slot_row_ref, slot_col_ref, ids_row_ref, ids_col_ref, proj_ref, weight_hbm,
    out_ref,
    weight, packed, arrived, attended, returned, own, pair_out, pair_in, far_out, far_in, kept,
    weight_sem, there_send, there_recv, back_send, back_recv, pair_send, pair_recv, far_send, far_recv,
):
    own_rows, columns = proj_ref.shape[1], proj_ref.shape[2]
    chunks, positions, _ = packed.shape
    capacity = positions // senders
    width = heads_step * HD
    block = out_ref.shape[1]
    pieces, tile = far_out.shape[0], far_out.shape[2]
    me = lax.axis_index("dp")
    rank = lax.axis_index("tensor")
    pair = (rank // 2) * 2 + (1 - rank % 2)
    far = (1 - rank // 2) * 2 + rank % 2
    masks = list(range(senders // 2, senders)) + list(range(senders // 2 - 1, 0, -1))

    fetch = pltpu.make_async_copy(weight_hbm, weight, weight_sem)
    fetch.start()
    barrier = pltpu.get_barrier_semaphore()
    for mask in masks:
        pl.semaphore_signal(barrier, inc=1, device_id=(xor(me, mask, senders), rank), device_id_type=pl.DeviceIdType.MESH)
    for other in (pair, far):
        pl.semaphore_signal(barrier, inc=1, device_id=(me, other), device_id_type=pl.DeviceIdType.MESH)
    pl.semaphore_wait(barrier, len(masks) + 2)

    def rows_of(device):
        return pl.ds(pl.multiple_of(device * capacity, capacity), capacity)

    def exchange(source, target, send_sem, recv_sem, chunk, mask):
        peer = xor(me, mask, senders)
        return pltpu.make_async_remote_copy(
            src_ref=source.at[chunk, rows_of(peer)],
            dst_ref=target.at[chunk, rows_of(me)],
            send_sem=send_sem.at[chunk, mask],
            recv_sem=recv_sem.at[chunk, mask],
            device_id=(peer, rank),
            device_id_type=pl.DeviceIdType.MESH,
        )

    def arrival(source, target, send_sem, recv_sem, chunk, mask):
        peer = xor(me, mask, senders)
        return pltpu.make_async_remote_copy(
            src_ref=source.at[chunk, rows_of(me)],
            dst_ref=target.at[chunk, rows_of(peer)],
            send_sem=send_sem.at[chunk, mask],
            recv_sem=recv_sem.at[chunk, mask],
            device_id=(peer, rank),
            device_id_type=pl.DeviceIdType.MESH,
        )

    there = (packed, arrived, there_send, there_recv)
    back = (attended, returned, back_send, back_recv)

    place = lax.broadcasted_iota(jnp.int32, (positions, own_rows), 0) == slot_row_ref[...]
    place = place.astype(jnp.float32).astype(jnp.bfloat16)
    for chunk in range(chunks):
        for part in range(3):
            piece = proj_ref[part, :, chunk * width:(chunk + 1) * width]
            packed[chunk, :, part * width:(part + 1) * width] = jnp.dot(
                place, piece, preferred_element_type=jnp.float32
            ).astype(jnp.bfloat16)
        for mask in masks:
            exchange(*there, chunk, mask).start()
        arrived[chunk, rows_of(me)] = packed[chunk, rows_of(me)]

    scale = 1.0 / math.sqrt(HD)
    for chunk in range(chunks):
        for mask in masks:
            arrival(*there, chunk, mask).wait_recv()
        for head in range(heads_step):
            at = head * HD
            query = arrived[chunk, :, at:at + HD]
            key = arrived[chunk, :, width + at:width + at + HD]
            value = arrived[chunk, :, 2 * width + at:2 * width + at + HD]
            scores = lax.dot_general(query, key, (((1,), (1,)), ((), ())), preferred_element_type=jnp.float32) * scale
            scores = jnp.where(ids_col_ref[...] == ids_row_ref[...], scores, -jnp.inf)
            raised = jnp.exp(scores - jnp.max(scores, axis=1, keepdims=True))
            weights = (raised / jnp.sum(raised, axis=1, keepdims=True)).astype(jnp.bfloat16)
            attended[chunk, :, at:at + HD] = jnp.dot(
                weights, value, preferred_element_type=jnp.float32
            ).astype(jnp.bfloat16)
        for mask in masks:
            exchange(*back, chunk, mask).start()
        returned[chunk, rows_of(me)] = attended[chunk, rows_of(me)]

    unplace = slot_col_ref[...] == lax.broadcasted_iota(jnp.int32, (own_rows, positions), 1)
    unplace = unplace.astype(jnp.float32).astype(jnp.bfloat16)
    for chunk in range(chunks):
        for mask in masks:
            arrival(*back, chunk, mask).wait_recv()
        own[:, chunk * width:(chunk + 1) * width] = jnp.dot(
            unplace, returned[chunk], preferred_element_type=jnp.float32
        ).astype(jnp.bfloat16)

    fetch.wait()

    def product(target, piece):
        start = pl.multiple_of(target * block + piece * tile, tile)
        return jnp.dot(own[...], weight[:, pl.ds(start, tile)], preferred_element_type=jnp.float32)

    def to_pair(side, piece):
        return pltpu.make_async_remote_copy(
            src_ref=pair_out.at[side, piece],
            dst_ref=pair_in.at[side, piece],
            send_sem=pair_send.at[side, piece],
            recv_sem=pair_recv.at[side, piece],
            device_id=(me, pair),
            device_id_type=pl.DeviceIdType.MESH,
        )

    def to_far(piece):
        return pltpu.make_async_remote_copy(
            src_ref=far_out.at[piece],
            dst_ref=far_in.at[piece],
            send_sem=far_send.at[piece],
            recv_sem=far_recv.at[piece],
            device_id=(me, far),
            device_id_type=pl.DeviceIdType.MESH,
        )

    far_of_pair = (1 - rank // 2) * 2 + (1 - rank % 2)
    for piece in range(pieces):
        pair_out[0, piece] = product(far_of_pair, piece).astype(jnp.bfloat16)
        to_pair(0, piece).start()
        mine = product(far, piece)
        to_pair(0, piece).wait_recv()
        far_out[piece] = (mine + pair_in[0, piece].astype(jnp.float32)).astype(jnp.bfloat16)
        to_far(piece).start()
    for piece in range(pieces):
        pair_out[1, piece] = product(pair, piece).astype(jnp.bfloat16)
        to_pair(1, piece).start()
        mine = product(rank, piece)
        to_pair(1, piece).wait_recv()
        kept[piece] = mine + pair_in[1, piece].astype(jnp.float32)
    for piece in range(pieces):
        to_far(piece).wait_recv()
        out_ref[:, piece * tile:(piece + 1) * tile] = (
            kept[piece] + far_in[piece].astype(jnp.float32)
        ).astype(out_ref.dtype)

    for chunk in range(chunks):
        for mask in masks:
            exchange(*there, chunk, mask).wait_send()
            exchange(*back, chunk, mask).wait_send()
    for piece in range(pieces):
        for side in range(2):
            to_pair(side, piece).wait_send()
        to_far(piece).wait_send()


def local_fused(projections, routes, segments, out_weight):
    senders = lax.axis_size("dp")
    ranks = lax.axis_size("tensor")
    own_rows, _, columns = projections.shape
    positions = segments.shape[1]
    capacity = positions // senders
    width_out = out_weight.shape[1]
    block = width_out // ranks
    heads_step = 2 if (columns // HD) % 2 == 0 else 1
    width = heads_step * HD
    chunks = columns // width
    pieces = block // 512
    slot_of_row, group_ids = routing(routes, segments, own_rows, senders, capacity)
    bf16, f32 = jnp.bfloat16, jnp.float32
    vmem = pl.BlockSpec(memory_space=pltpu.VMEM)
    return pl.pallas_call(
        functools.partial(fused_kernel, senders, heads_step),
        out_shape=jax.ShapeDtypeStruct((own_rows, block), bf16),
        in_specs=[vmem] * 5 + [pl.BlockSpec(memory_space=pl.ANY)],
        out_specs=vmem,
        scratch_shapes=[
            pltpu.VMEM((columns, width_out), bf16),
            pltpu.VMEM((chunks, positions, 3 * width), bf16),
            pltpu.VMEM((chunks, positions, 3 * width), bf16),
            pltpu.VMEM((chunks, positions, width), bf16),
            pltpu.VMEM((chunks, positions, width), bf16),
            pltpu.VMEM((own_rows, columns), bf16),
            pltpu.VMEM((2, pieces, own_rows, 512), bf16),
            pltpu.VMEM((2, pieces, own_rows, 512), bf16),
            pltpu.VMEM((pieces, own_rows, 512), bf16),
            pltpu.VMEM((pieces, own_rows, 512), bf16),
            pltpu.VMEM((pieces, own_rows, 512), f32),
            pltpu.SemaphoreType.DMA(()),
            pltpu.SemaphoreType.DMA((chunks, senders)),
            pltpu.SemaphoreType.DMA((chunks, senders)),
            pltpu.SemaphoreType.DMA((chunks, senders)),
            pltpu.SemaphoreType.DMA((chunks, senders)),
            pltpu.SemaphoreType.DMA((2, pieces)),
            pltpu.SemaphoreType.DMA((2, pieces)),
            pltpu.SemaphoreType.DMA((pieces,)),
            pltpu.SemaphoreType.DMA((pieces,)),
        ],
        compiler_params=pltpu.CompilerParams(
            collective_id=0, has_side_effects=True, vmem_limit_bytes=50 * 2**20
        ),
    )(
        slot_of_row[None, :], slot_of_row[:, None], group_ids[None, :], group_ids[:, None],
        jnp.transpose(projections, (1, 0, 2)), out_weight,
    )


def solution(mesh):
    in_specs = (P("dp", None, "tensor"), P(), P("dp", None), P("tensor", None))
    out_specs = P("dp", "tensor")
    senders, ranks = mesh.shape["dp"], mesh.shape["tensor"]

    def program(projections, routes, segments, out_weight):
        capacity = segments.shape[1] // senders
        fused = (
            ranks == 4
            and senders & (senders - 1) == 0
            and capacity % 16 == 0
            and (out_weight.shape[1] // ranks) % 512 == 0
        )
        body = jax.shard_map(
            local_fused if fused else local, mesh=mesh, in_specs=in_specs, out_specs=out_specs, check_vma=False
        )
        return body(projections, routes, segments, out_weight)

    return program
```

```python
import functools
import math

import jax
import jax.numpy as jnp
from jax import lax
from jax.experimental import pallas as pl
from jax.experimental.pallas import tpu as pltpu
from jax.sharding import PartitionSpec as P

HD = 128
SPLITS = 4


def routing(routes, segments, own_rows, senders, capacity):
    positions = senders * capacity
    myself = lax.axis_index("dp")
    targets = routes[:, 0]
    mine = lax.dynamic_slice_in_dim(targets, myself * own_rows, own_rows)
    row = jnp.arange(own_rows, dtype=jnp.int32)
    same_before = (mine[:, None] == mine[None, :]) & (row[None, :] < row[:, None])
    slot_of_row = mine * capacity + jnp.sum(same_before.astype(jnp.int32), axis=1)
    arrivals = jnp.sum((targets.reshape(senders, own_rows) == myself).astype(jnp.int32), axis=1)
    device = jnp.arange(senders, dtype=jnp.int32)
    earlier = jnp.sum(jnp.where(device[None, :] < device[:, None], arrivals[None, :], 0), axis=1)
    within = jnp.arange(capacity, dtype=jnp.int32)
    placed = (earlier[:, None] + within[None, :]).reshape(positions)
    filled = (within[None, :] < arrivals[:, None]).reshape(positions)
    flat = jnp.arange(positions, dtype=jnp.int32)
    looked_up = jnp.sum(jnp.where(placed[:, None] == flat[None, :], segments[0][None, :], 0), axis=1)
    return slot_of_row, jnp.where(filled, looked_up, -1 - flat)


def attend_heads(arrived, group_ids):
    slot_total, _, heads_now, head_size = arrived.shape
    block_rows = min(slot_total, 512)
    block_count = slot_total // block_rows
    queries = arrived[:, 0].reshape(block_count, block_rows, heads_now, head_size)
    query_ids = group_ids.reshape(block_count, block_rows)
    keys_in, values_in = arrived[:, 1], arrived[:, 2]
    scale = 1.0 / math.sqrt(head_size)

    def one_block(block_pair):
        query_block, ids = block_pair
        scores = jnp.einsum("qhd,khd->hqk", query_block, keys_in, preferred_element_type=jnp.float32) * scale
        scores = jnp.where((ids[:, None] == group_ids[None, :])[None], scores, -jnp.inf)
        raised = jnp.exp(scores - jnp.max(scores, axis=2, keepdims=True))
        weights = (raised / jnp.sum(raised, axis=2, keepdims=True)).astype(jnp.bfloat16)
        return jnp.einsum("hqk,khd->qhd", weights, values_in, preferred_element_type=jnp.float32).astype(jnp.bfloat16)

    return lax.map(one_block, (queries, query_ids)).reshape(slot_total, heads_now * head_size)


def local(projections, routes, segments, out_weight):
    senders = lax.axis_size("dp")
    own_rows, _, columns = projections.shape
    heads_here = columns // HD
    positions = segments.shape[1]
    capacity = positions // senders
    slot_of_row, group_ids = routing(routes, segments, own_rows, senders, capacity)
    source_row = jnp.zeros((positions,), jnp.int32).at[slot_of_row].set(jnp.arange(own_rows, dtype=jnp.int32))
    outgoing = projections[source_row].reshape(senders, capacity, 3, heads_here, HD)
    arrived = lax.all_to_all(outgoing, "dp", split_axis=0, concat_axis=0, tiled=True)
    attended = attend_heads(arrived.reshape(positions, 3, heads_here, HD), group_ids)
    returned = lax.all_to_all(
        attended.reshape(senders, capacity, columns), "dp", split_axis=0, concat_axis=0, tiled=True
    )
    own = returned.reshape(positions, columns)[slot_of_row]
    partial_value = jnp.dot(own, out_weight, preferred_element_type=jnp.float32)
    return lax.psum_scatter(partial_value.astype(jnp.bfloat16), "tensor", scatter_dimension=1, tiled=True)


def xor(index, mask, size):
    result, bit = 0, 1
    while bit < size:
        digit = (index // bit) % 2
        result = result + ((1 - digit) if (mask // bit) % 2 else digit) * bit
        bit *= 2
    return result


def fused_kernel(
    senders, splits, heads_step,
    slot_row_ref, turn_row_ref, turn_col_ref, ids_row_ref, ids_col_ref, proj_ref, weight_hbm,
    out_ref,
    weight, packed_q, arrived_q, packed_kv, arrived_kv, attended, returned,
    pair_out, pair_in, far_out, far_in, kept, summed,
    weight_sem, q_send, q_recv, kv_send, kv_recv, back_send, back_recv, pair_send, pair_recv, far_send, far_recv,
):
    own_rows, columns = proj_ref.shape[1], proj_ref.shape[2]
    chunks, positions, _ = packed_kv.shape
    capacity = positions // senders
    sub = capacity // splits
    rows = senders * sub
    width = heads_step * HD
    block = out_ref.shape[1]
    me = lax.axis_index("dp")
    rank = lax.axis_index("tensor")
    pair = (rank // 2) * 2 + (1 - rank % 2)
    far = (1 - rank // 2) * 2 + rank % 2
    far_of_pair = (1 - rank // 2) * 2 + (1 - rank % 2)
    masks = list(range(senders // 2, senders)) + list(range(senders // 2 - 1, 0, -1))
    f32, bf16 = jnp.float32, jnp.bfloat16

    fetch = pltpu.make_async_copy(weight_hbm, weight, weight_sem)
    fetch.start()
    barrier = pltpu.get_barrier_semaphore()
    for mask in masks:
        pl.semaphore_signal(barrier, inc=1, device_id=(xor(me, mask, senders), rank), device_id_type=pl.DeviceIdType.MESH)
    for other in (pair, far):
        pl.semaphore_signal(barrier, inc=1, device_id=(me, other), device_id_type=pl.DeviceIdType.MESH)
    pl.semaphore_wait(barrier, len(masks) + 2)

    def rows_of(device, size):
        return pl.ds(pl.multiple_of(device * size, size), size)

    def copy(kind, at, mask, arriving=False):
        source, target, send_sem, recv_sem, size = kind
        peer = xor(me, mask, senders)
        first, second = (me, peer) if arriving else (peer, me)
        return pltpu.make_async_remote_copy(
            src_ref=source.at[at, rows_of(first, size)],
            dst_ref=target.at[at, rows_of(second, size)],
            send_sem=send_sem.at[at, mask],
            recv_sem=recv_sem.at[at, mask],
            device_id=(peer, rank),
            device_id_type=pl.DeviceIdType.MESH,
        )

    def send(kind, at):
        source, target, _, _, size = kind
        for mask in masks:
            copy(kind, at, mask).start()
        target[at, rows_of(me, size)] = source[at, rows_of(me, size)]

    def receive(kind, at):
        for mask in masks:
            copy(kind, at, mask, arriving=True).wait_recv()

    queries = (packed_q, arrived_q, q_send, q_recv, sub)
    pairs = (packed_kv, arrived_kv, kv_send, kv_recv, capacity)
    back = (attended, returned, back_send, back_recv, sub)

    def one_hot(count, targets):
        hits = lax.broadcasted_iota(jnp.int32, (count, own_rows), 0) == targets
        return hits.astype(f32).astype(bf16)

    def pick(matrix, piece):
        return jnp.dot(matrix, piece, preferred_element_type=f32).astype(bf16)

    def pack_queries(split):
        packed_q[split] = pick(one_hot(rows, turn_row_ref[...] - split * rows), proj_ref[0])

    pack_queries(0)
    send(queries, 0)
    place = one_hot(positions, slot_row_ref[...])
    for chunk in range(chunks):
        for part in range(2):
            packed_kv[chunk, :, part * width:(part + 1) * width] = pick(
                place, proj_ref[1 + part, :, chunk * width:(chunk + 1) * width]
            )
        send(pairs, chunk)
    for split in range(1, splits):
        pack_queries(split)
    ahead = min(2, splits)
    for split in range(1, ahead):
        send(queries, split)

    scale = 1.0 / math.sqrt(HD)

    def attend(split):
        receive(queries, split)
        allowed = ids_col_ref[split * rows:(split + 1) * rows] == ids_row_ref[...]
        for chunk in range(chunks):
            if split == 0:
                receive(pairs, chunk)
            for head in range(heads_step):
                at = head * HD
                column = chunk * width + at
                query = arrived_q[split, :, column:column + HD]
                key = arrived_kv[chunk, :, at:at + HD]
                value = arrived_kv[chunk, :, width + at:width + at + HD]
                scores = lax.dot_general(query, key, (((1,), (1,)), ((), ())), preferred_element_type=f32) * scale
                scores = jnp.where(allowed, scores, -jnp.inf)
                raised = jnp.exp(scores - jnp.max(scores, axis=1, keepdims=True))
                weights = (raised / jnp.sum(raised, axis=1, keepdims=True)).astype(bf16)
                attended[split, :, column:column + HD] = pick(weights, value)
        send(back, split)
        if split + ahead < splits:
            send(queries, split + ahead)

    def product(split, target):
        start = pl.multiple_of(target * block, block)
        return jnp.dot(returned[split], weight[:, pl.ds(start, block)], preferred_element_type=f32)

    def to_pair(side, split):
        return pltpu.make_async_remote_copy(
            src_ref=pair_out.at[side, split],
            dst_ref=pair_in.at[side, split],
            send_sem=pair_send.at[side, split],
            recv_sem=pair_recv.at[side, split],
            device_id=(me, pair),
            device_id_type=pl.DeviceIdType.MESH,
        )

    def to_far(split):
        return pltpu.make_async_remote_copy(
            src_ref=far_out.at[split],
            dst_ref=far_in.at[split],
            send_sem=far_send.at[split],
            recv_sem=far_recv.at[split],
            device_id=(me, far),
            device_id_type=pl.DeviceIdType.MESH,
        )

    def project(split):
        receive(back, split)
        if split == 0:
            fetch.wait()
        pair_out[0, split] = product(split, far_of_pair).astype(bf16)
        to_pair(0, split).start()
        mine = product(split, far)
        to_pair(0, split).wait_recv()
        far_out[split] = (mine + pair_in[0, split].astype(f32)).astype(bf16)
        to_far(split).start()
        pair_out[1, split] = product(split, pair).astype(bf16)
        to_pair(1, split).start()
        kept[split] = product(split, rank)

    for split in range(splits):
        attend(split)
        if split >= 1:
            project(split - 1)
    project(splits - 1)
    for split in range(splits):
        to_pair(1, split).wait_recv()
        total = kept[split] + pair_in[1, split].astype(f32)
        to_far(split).wait_recv()
        summed[split * rows:(split + 1) * rows] = (total + far_in[split].astype(f32)).astype(bf16)
    unplace = turn_col_ref[...] == lax.broadcasted_iota(jnp.int32, (own_rows, positions), 1)
    out_ref[...] = pick(unplace.astype(f32).astype(bf16), summed[...])

    for mask in masks:
        for chunk in range(chunks):
            copy(pairs, chunk, mask).wait_send()
        for split in range(splits):
            copy(queries, split, mask).wait_send()
            copy(back, split, mask).wait_send()
    for split in range(splits):
        to_pair(0, split).wait_send()
        to_pair(1, split).wait_send()
        to_far(split).wait_send()


def local_fused(projections, routes, segments, out_weight):
    senders = lax.axis_size("dp")
    ranks = lax.axis_size("tensor")
    own_rows, _, columns = projections.shape
    positions = segments.shape[1]
    capacity = positions // senders
    width_out = out_weight.shape[1]
    block = width_out // ranks
    heads_step = 2 if (columns // HD) % 2 == 0 else 1
    width = heads_step * HD
    chunks = columns // width
    splits = SPLITS if capacity % (16 * SPLITS) == 0 else 1
    sub = capacity // splits
    rows = senders * sub
    slot_of_row, group_ids = routing(routes, segments, own_rows, senders, capacity)
    turn = ((slot_of_row % capacity) // sub) * rows + (slot_of_row // capacity) * sub + slot_of_row % sub
    ids_turned = group_ids.reshape(senders, splits, sub).transpose(1, 0, 2).reshape(positions, 1)
    bf16, f32 = jnp.bfloat16, jnp.float32
    vmem = pl.BlockSpec(memory_space=pltpu.VMEM)
    dma = pltpu.SemaphoreType.DMA
    return pl.pallas_call(
        functools.partial(fused_kernel, senders, splits, heads_step),
        out_shape=jax.ShapeDtypeStruct((own_rows, block), bf16),
        in_specs=[vmem] * 6 + [pl.BlockSpec(memory_space=pl.ANY)],
        out_specs=vmem,
        scratch_shapes=[
            pltpu.VMEM((columns, width_out), bf16),
            pltpu.VMEM((splits, rows, columns), bf16),
            pltpu.VMEM((splits, rows, columns), bf16),
            pltpu.VMEM((chunks, positions, 2 * width), bf16),
            pltpu.VMEM((chunks, positions, 2 * width), bf16),
            pltpu.VMEM((splits, rows, columns), bf16),
            pltpu.VMEM((splits, rows, columns), bf16),
            pltpu.VMEM((2, splits, rows, block), bf16),
            pltpu.VMEM((2, splits, rows, block), bf16),
            pltpu.VMEM((splits, rows, block), bf16),
            pltpu.VMEM((splits, rows, block), bf16),
            pltpu.VMEM((splits, rows, block), f32),
            pltpu.VMEM((positions, block), bf16),
            dma(()),
            dma((splits, senders)),
            dma((splits, senders)),
            dma((chunks, senders)),
            dma((chunks, senders)),
            dma((splits, senders)),
            dma((splits, senders)),
            dma((2, splits)),
            dma((2, splits)),
            dma((splits,)),
            dma((splits,)),
        ],
        compiler_params=pltpu.CompilerParams(
            collective_id=0, has_side_effects=True, vmem_limit_bytes=50 * 2**20
        ),
    )(
        slot_of_row[None, :], turn[None, :], turn[:, None], group_ids[None, :], ids_turned,
        jnp.transpose(projections, (1, 0, 2)), out_weight,
    )


def solution(mesh):
    in_specs = (P("dp", None, "tensor"), P(), P("dp", None), P("tensor", None))
    out_specs = P("dp", "tensor")
    senders, ranks = mesh.shape["dp"], mesh.shape["tensor"]

    def program(projections, routes, segments, out_weight):
        capacity = segments.shape[1] // senders
        fused = (
            ranks == 4
            and senders & (senders - 1) == 0
            and capacity % 16 == 0
            and (out_weight.shape[1] // ranks) % 512 == 0
        )
        body = jax.shard_map(
            local_fused if fused else local, mesh=mesh, in_specs=in_specs, out_specs=out_specs, check_vma=False
        )
        return body(projections, routes, segments, out_weight)

    return program
```
